32 devices in a mesh: leaf: 4 (over x, core), blk: 8 (over z, y).
Axes of the slice: x: 2, y: 2, z: 4, core: 2. Of those that a mesh axis runs over, the one named last changes fastest.
Arguments:
- interior_factor: float32 [32, 256, 256], P(('leaf', 'blk')), may hold values from -0.375 to 0.375
- coupling: float32 [32, 64, 256], P(('leaf', 'blk')), may hold values from -2 to 2
- iface_rows: int32 [32, 64], P(('leaf', 'blk')), may hold values from 0 to 1535, as said below
- counts: int32 [32], P(('leaf', 'blk')), may hold values from 16 to 64, as said below
- resid_interior: float32 [32, 256], P(('leaf', 'blk')), may hold values from -6 to 6
- resid_iface: float32 [1536], replicated, may hold values from -6 to 6
- iface_operator: float32 [1536, 1536], replicated, as said below
Outputs:
- interior_solution: float32 [32, 256], P(('leaf', 'blk'))
- iface_solution: float32 [1536], P('blk')
The draws below stay inside these ranges and needn't reach their ends.
Inputs may be any that keep to these rules, and one draw needn't show every extreme that they name: `iface_rows`: the 64 rows of one block's list are distinct. `counts`: some block uses 64 rows and some block uses 64 // 4. `iface_operator`: symmetric positive definite.
All inputs are finite; a program needn't handle non-finite values.
Results may differ from the reference program's by a relative error of at most 0.0002.
Values sent between devices are 32-bit elements; how exact they have to be, the bound alone decides.
No kernel may reach another device: no remote copies, remote signals or barrier semaphores. Data moves between devices by JAX's collectives and lax.ppermute only.
A program may use at most 128 MiB of HBM per device.

```python
import math
import jax
import jax.numpy as jnp
from jax import lax

S = 1536
CMAX = 64
NI = 256
BLOCKS = 32


def one_list(block_key):
    return jax.random.permutation(block_key, S)[:CMAX]


def draw_iface_rows(key, part):
    key = jax.random.fold_in(key, 11)
    block_keys = jax.random.split(key, BLOCKS)
    return jax.vmap(one_list)(block_keys).astype(jnp.int32)


def draw_counts(key, part):
    key = jax.random.fold_in(key, 12)
    key_one, key_two, key_three = jax.random.split(key, 3)
    drawn = jax.random.randint(key_one, (BLOCKS,), CMAX // 4, CMAX + 1)
    high_spot = jax.random.randint(key_two, (), 0, BLOCKS)
    offset = jax.random.randint(key_three, (), 1, BLOCKS)
    low_spot = (high_spot + offset) % BLOCKS
    position = jnp.arange(BLOCKS)
    drawn = jnp.where(position == high_spot, CMAX, drawn)
    drawn = jnp.where(position == low_spot, CMAX // 4, drawn)
    return drawn.astype(jnp.int32)


def draw_coupling(key, part):
    key = jax.random.fold_in(key, 14)
    key_one, key_two, key_three = jax.random.split(key, 3)
    overall = math.sqrt(3.0 * S / (NI * CMAX * BLOCKS))
    gains = jnp.exp(jax.random.uniform(key_three, (BLOCKS, CMAX, 1), jnp.float32, math.log(0.5), math.log(2.0)))
    common_share, single_share = (0.8, 0.6)
    common = jax.random.truncated_normal(key_one, -4.0, 4.0, (BLOCKS, 1, NI), jnp.float32)
    single = jax.random.truncated_normal(key_two, -4.0, 4.0, (BLOCKS, CMAX, NI), jnp.float32)
    return overall * (common_share * gains * common + single_share * single)


def draw_iface_operator(key, part):
    key = jax.random.fold_in(key, 13)
    key_one, key_two, key_three = jax.random.split(key, 3)
    weight_low, weight_high, margin_low, margin_high = (0.5, 1.5, 0.001, 0.003)
    position = jnp.arange(S)
    column = position % 32
    weight_across = jax.random.uniform(key_one, (S,), jnp.float32, weight_low, weight_high)
    weight_across = jnp.where(column < 31, weight_across, 0.0)
    weight_below = jax.random.uniform(key_two, (S,), jnp.float32, weight_low, weight_high)
    weight_below = jnp.where(position < S - 32, weight_below, 0.0)
    margins = jax.random.uniform(key_three, (S,), jnp.float32, margin_low, margin_high)
    left_edge = jnp.concatenate([jnp.zeros((1,), jnp.float32), weight_across[:-1]])
    upper_edge = jnp.concatenate([jnp.zeros((32,), jnp.float32), weight_below[:-32]])
    row_index = position[:, None]
    col_index = position[None, :]
    off_part = weight_across[:, None] * (col_index == row_index + 1).astype(jnp.float32)
    off_part = off_part + weight_across[None, :] * (row_index == col_index + 1).astype(jnp.float32)
    off_part = off_part + weight_below[:, None] * (col_index == row_index + 32).astype(jnp.float32)
    off_part = off_part + weight_below[None, :] * (row_index == col_index + 32).astype(jnp.float32)
    diagonal = weight_across + left_edge + weight_below + upper_edge + margins
    on_diagonal = (row_index == col_index).astype(jnp.float32)
    return on_diagonal * diagonal[None, :] - off_part


def shard_levels(rng, dims, shards, smallest, high):
    loudness, own = 1.0, jax.random.fold_in(rng, 6)
    for axis_at, blocks in shards:
        draws = jnp.exp(jax.random.uniform(jax.random.fold_in(own, axis_at), (blocks,), jnp.float32, smallest / len(shards), high / len(shards)))
        loudness = loudness * jnp.repeat(draws, dims[axis_at] // blocks).reshape([-1 if axis == axis_at else 1 for axis in range(len(dims))])
    return loudness


def scatter_about(key, extent, width, bound, cuts=(), kind=jnp.bfloat16):
    values = width * jax.random.normal(key, extent, jnp.float32)
    if cuts:
        values = values * shard_levels(key, extent, cuts, -0.22, 0.18)
    return jnp.clip(values, -bound, bound).astype(kind)


def setup_inputs(seed: int = 0) -> dict:
    key_of = jax.random.split(jax.random.key(seed), 8)
    interior_factor = scatter_about(key_of[0], (BLOCKS, NI, NI), NI ** -0.5, 0.375, ((0, 32),), jnp.float32)
    coupling = draw_coupling(jax.random.fold_in(key_of[7], 71), 0)
    iface_rows = draw_iface_rows(jax.random.fold_in(key_of[7], 71), 0)
    counts = draw_counts(jax.random.fold_in(key_of[7], 71), 0)
    resid_interior = scatter_about(key_of[4], (BLOCKS, NI), 1.0, 6.0, ((0, 32),), jnp.float32)
    resid_iface = scatter_about(key_of[5], (S,), 1.0, 6.0, (), jnp.float32)
    iface_operator = draw_iface_operator(jax.random.fold_in(key_of[7], 71), 0)
    return dict(interior_factor=interior_factor, coupling=coupling, iface_rows=iface_rows, counts=counts, resid_interior=resid_interior, resid_iface=resid_iface, iface_operator=iface_operator)


def reference(interior_factor, coupling, iface_rows, counts, resid_interior, resid_iface, iface_operator):
    highest = lax.Precision.HIGHEST
    active = (jnp.arange(CMAX, dtype=jnp.int32)[None, :] < counts[:, None]).astype(jnp.float32)
    coupled = coupling * active[:, :, None]
    reduced = jnp.einsum('kcn,kmn->kcm', coupled, interior_factor, precision=highest)
    local_rhs = jnp.einsum('kmn,kn->km', interior_factor, resid_interior, precision=highest)
    pieces = jnp.einsum('kcm,kdm->kcd', reduced, reduced, precision=highest)
    piece_rhs = jnp.einsum('kcm,km->kc', reduced, local_rhs, precision=highest)
    schur_matrix = iface_operator.at[iface_rows[:, :, None], iface_rows[:, None, :]].add(pieces)
    iface_rhs = resid_iface.at[iface_rows].add(piece_rhs)
    lower_factor = jnp.linalg.cholesky(schur_matrix)
    solution = jax.scipy.linalg.cho_solve((lower_factor, True), iface_rhs)
    picked = solution[iface_rows]
    corrected = resid_interior - jnp.einsum('kc,kcn->kn', picked, coupled, precision=highest)
    inner_values = jnp.einsum('kmn,kn->km', interior_factor, corrected, precision=highest)
    interior = jnp.einsum('kmn,km->kn', interior_factor, inner_values, precision=highest)
    return (interior, solution)
```

```python
import functools
import jax
import jax.numpy as jnp
from jax import lax
from jax.experimental import pallas as pl
from jax.experimental.pallas import tpu as pltpu
from jax.sharding import PartitionSpec as P

F32 = jnp.float32
BF16 = jnp.bfloat16
HIGHEST = lax.Precision.HIGHEST
NB = 128
TB = 256
NT = (((1,), (1,)), ((), ()))


def lane_of(x, j):
    return jnp.broadcast_to(x[:, j : j + 1], (8, 128))


def row_of(x, i):
    return jnp.broadcast_to(x[i : i + 1, :], (8, 128))


def split(x):
    high = x.astype(BF16)
    return high, (x - high.astype(F32)).astype(BF16)


def first_factors(x):
    high, low = split(x)
    return jnp.concatenate([high, high, low], axis=1)


def second_factors(x):
    high, low = split(x)
    return jnp.concatenate([high, low, high], axis=1)


def product(a, b):
    return lax.dot_general(a, b, NT, preferred_element_type=F32)


def inverse_root(T):
    T = list(T)
    groups = len(T)
    lane = lax.broadcasted_iota(jnp.int32, (8, 128), 1)
    sub = lax.broadcasted_iota(jnp.int32, (8, 128), 0)
    zero = jnp.zeros((8, 128), F32)
    W = [None] * groups

    def corner(columns):
        return [[row_of(columns[j], i) if i >= j else None for j in range(8)] for i in range(8)]

    G = corner([lane_of(T[0], j) for j in range(8)])
    after = [lane_of(T[1], j) for j in range(8)]
    ahead = [lane_of(T[1], 8 + j) for j in range(8)]
    for g in range(groups):
        last = g == groups - 1
        inside = (lane >= 8 * g) & (lane < 8 * g + 8)
        t = [jnp.where(inside, jnp.where(lane == 8 * g + j, 1.0, 0.0), row_of(T[g], j)) for j in range(8)]
        r = [None] * 8
        f = [[None] * 8 for _ in range(8)]
        if not last:
            following = jnp.where(inside, zero, T[g + 1])
        for p in range(8):
            r[p] = 1.0 / G[p][p]
            for j in range(p + 1, 8):
                f[j][p] = G[j][p] * r[p]
            for j in range(p + 1, 8):
                for k in range(p + 1, j + 1):
                    G[j][k] = G[j][k] - f[j][p] * G[k][p]
            for j in range(p + 1, 8):
                t[j] = t[j] - f[j][p] * t[p]
            if not last:
                scaled = after[p] * r[p]
                for j in range(8):
                    ahead[j] = ahead[j] - scaled * row_of(after[p], j)
                for k in range(p + 1, 8):
                    after[k] = after[k] - scaled * G[k][p]
                following = following - scaled * t[p]
        w = zero
        for p in range(8):
            w = jnp.where(sub == p, t[p] * jnp.sqrt(r[p]), w)
        W[g] = jnp.where(lane < 8 * g + 8, w, 0.0)
        if last:
            break
        T[g + 1] = following
        G = corner(ahead)
        if g + 2 < groups:
            e = [None] * 8
            for p in reversed(range(8)):
                e[p] = t[p] * r[p]
                for k in range(p + 1, 8):
                    e[p] = e[p] - f[k][p] * e[k]
            for i in range(g + 2, groups):
                old = T[i]
                T[i] = jnp.where(inside, zero, old)
                for j in range(8):
                    T[i] = T[i] - lane_of(old, 8 * g + j) * e[j]
            after = [lane_of(T[g + 2], 8 * (g + 1) + j) for j in range(8)]
            ahead = [lane_of(T[g + 2], 8 * (g + 2) + j) for j in range(8)]
    return W


def piece_kernel(count_ref, coupling_ref, factor_ref, resid_ref, rows_ref, out_ref):
    capacity, interior = coupling_ref.shape
    active = lax.broadcasted_iota(jnp.int32, (capacity, interior), 0) < count_ref[0]
    coupled = jnp.where(active, coupling_ref[...], 0.0)
    extra = jnp.broadcast_to(resid_ref[...], (8, interior))
    both = jnp.concatenate([coupled, extra], axis=0)
    reduced = lax.dot_general(both, factor_ref[...], NT, precision=HIGHEST, preferred_element_type=F32)
    square = lax.dot_general(reduced, reduced[:capacity], NT, precision=HIGHEST, preferred_element_type=F32)
    half = capacity // 2
    out_ref[0:half, 0:capacity] = square[0:half]
    out_ref[0:half, capacity : 2 * capacity] = square[half:capacity]
    out_ref[half : half + 8, 0:capacity] = square[capacity : capacity + 8]
    out_ref[half : half + 8, capacity : 2 * capacity] = jnp.broadcast_to(
        rows_ref[...].astype(F32), (8, capacity)
    )


def system_kernel(
    steps,
    n,
    me_ref,
    own_rows_ref,
    count_ref,
    pieces_ref,
    operator_ref,
    resid_iface_ref,
    coupling_ref,
    factor_ref,
    resid_ref,
    interior_ref,
    iface_ref,
    M,
    by_row,
    z_rows,
    listed,
    listed_int,
    inverse,
    rhs,
    first,
    second,
    roots,
    x_columns,
    picked,
    listed_smem,
    sem_operator,
    sem_listed,
):
    S = M.shape[0]
    chunks = S // 128
    capacity = coupling_ref.shape[0]
    half = capacity // 2
    size = half + 8
    me = me_ref[0]
    lane = lax.broadcasted_iota(jnp.int32, (8, 128), 1)
    sub = lax.broadcasted_iota(jnp.int32, (8, 128), 0)

    get_operator = pltpu.make_async_copy(operator_ref, M, sem_operator)
    get_operator.start()

    def slot_of(k):
        bits = k ^ me
        slot = 0
        for t, bit in enumerate(steps):
            slot = slot + (((bits >> bit) & 1) << t)
        return slot

    def list_rows(k, carry):
        listed[pl.ds(k, 1), :] = pieces_ref[pl.ds(slot_of(k) * size + half, 1), :]
        return carry

    lax.fori_loop(0, n, list_rows, 0)
    listed_int[...] = listed[...].astype(jnp.int32)
    get_listed = pltpu.make_async_copy(listed_int, listed_smem, sem_listed)
    get_listed.start()

    def clear(i, carry):
        by_row[pl.ds(pl.multiple_of(i * 128, 128), 128), :] = jnp.zeros((128, 128), F32)
        return carry

    lax.fori_loop(0, by_row.shape[0] // 128, clear, 0)

    def invert(b, carry):
        rows8 = listed_int[pl.ds(pl.multiple_of(b * 8, 8), 8), :]
        found = [jnp.full((8, 128), -1, jnp.int32) for _ in range(chunks)]
        for i in range(capacity):
            target = lane_of(rows8, capacity + i)
            for c in range(chunks):
                found[c] = jnp.where(lane + 128 * c == target, i, found[c])
        for c in range(chunks):
            inverse[pl.ds(pl.multiple_of(c * n + b * 8, 8), 8), :] = found[c]
        return carry

    lax.fori_loop(0, n // 8, invert, 0)
    get_listed.wait()

    rhs[...] = jnp.broadcast_to(resid_iface_ref[...], rhs.shape)

    def scatter(k, carry):
        base = slot_of(k) * size
        strips = [pieces_ref[pl.ds(pl.multiple_of(base + 8 * s, 8), 8), :] for s in range(size // 8)]
        for c in range(chunks):
            at = jnp.broadcast_to(inverse[pl.ds(c * n + k, 1), :], (8, 128))
            member = at >= 0
            low = jnp.maximum(at, 0)
            high = low + capacity
            for s in range(half // 8):
                for which, index in ((0, low), (half, high)):
                    spread = jnp.take_along_axis(strips[s], index, axis=1, mode="promise_in_bounds")
                    z_rows[pl.ds((which + 8 * s) * 16 + c, 8, stride=16), :] = jnp.where(member, spread, 0.0)
            spread = jnp.take_along_axis(strips[half // 8], low, axis=1, mode="promise_in_bounds")
            spread = jnp.where(member, spread, 0.0)
            cols = slice(128 * c, 128 * (c + 1))
            rhs[0:8, cols] = rhs[0:8, cols] + spread
        for i in range(0, capacity, 8):
            places = [pl.multiple_of(listed_smem[k, capacity + i + u] * 16, 16) for u in range(8)]
            sums = [
                by_row[pl.ds(places[u], 16), :] + z_rows[16 * (i + u) : 16 * (i + u + 1), :] for u in range(8)
            ]
            for u in range(8):
                by_row[pl.ds(places[u], 16), :] = sums[u]
        return carry

    lax.fori_loop(0, n, scatter, 0)
    rhs[8:16, :] = rhs[0:8, :]
    get_operator.wait()

    def assemble(q, carry):
        row = pl.multiple_of(q * 8, 8)
        for c in range(chunks):
            cols = slice(128 * c, 128 * (c + 1))
            M[pl.ds(row, 8), cols] = M[pl.ds(row, 8), cols] + by_row[pl.ds(row * 16 + c, 8, stride=16), :]
        return carry

    lax.fori_loop(0, S // 8, assemble, 0)

    panels = S // NB
    tiles = S // TB

    def panel(j, carry):
        at = pl.multiple_of(j * NB, NB)
        here = pl.ds(at, NB)
        W = inverse_root([M[pl.ds(at + 8 * s, 8), here] for s in range(NB // 8)])
        W = jnp.concatenate(W, axis=0)
        roots[here, :] = W.T
        W_second = second_factors(W)
        z = product(first_factors(rhs[:, here]), W_second)
        rhs[:, here] = z
        z_first = first_factors(z)
        first[here, :] = jnp.zeros((NB, 3 * NB), BF16)
        second[here, :] = jnp.zeros((NB, 3 * NB), BF16)

        def column(i, carry):
            rows = pl.ds(pl.multiple_of(i * NB, NB), NB)
            V = product(first_factors(M[rows, here]), W_second)
            M[rows, here] = V
            first[rows, :] = first_factors(V)
            second[rows, :] = second_factors(V)
            return carry

        lax.fori_loop(j + 1, panels, column, 0)

        def across(b, carry):
            cols = pl.ds(pl.multiple_of(b * TB, TB), TB)
            weights = second[cols, :]
            rhs[:, cols] = rhs[:, cols] - product(z_first, weights)

            def down(a, carry):
                rows = pl.ds(pl.multiple_of(a * TB, TB), TB)
                M[rows, cols] = M[rows, cols] - product(first[rows, :], weights)
                return carry

            lax.fori_loop(b, tiles, down, 0)
            return carry

        @pl.when(j + 1 < panels)
        def _():
            lax.fori_loop((j + 1) // 2, tiles, across, 0)

        return carry

    lax.fori_loop(0, panels, panel, 0)

    def back(step, carry):
        j = panels - 1 - step
        at = pl.multiple_of(j * NB, NB)
        t = jnp.broadcast_to(rhs[0:1, pl.ds(at, NB)], (8, NB))
        x = []
        flat = jnp.zeros((8, 128), F32)
        for s in range(NB // 8):
            total = jnp.sum(roots[pl.ds(at + 8 * s, 8), :] * t, axis=1, keepdims=True)
            total = jnp.broadcast_to(total, (8, 128))
            x.append(total)
            x_columns[pl.ds(at + 8 * s, 8), :] = total
            flat = flat + jnp.where(lane == sub + 8 * s, total, 0.0)
        iface_ref[:, pl.ds(at, NB)] = jnp.sum(flat, axis=0, keepdims=True)
        for c in range(chunks):
            cols = slice(128 * c, 128 * (c + 1))
            total = x[0] * M[pl.ds(at, 8), cols]
            for s in range(1, NB // 8):
                total = total + x[s] * M[pl.ds(at + 8 * s, 8), cols]
            rhs[0:1, cols] = rhs[0:1, cols] - jnp.sum(total, axis=0, keepdims=True)
        return carry

    lax.fori_loop(0, panels, back, 0)

    for i in range(capacity):
        picked[i : i + 1, :] = x_columns[pl.ds(own_rows_ref[0, i], 1), :]
    interior = coupling_ref.shape[1]
    corrected = []
    for c in range(interior // 128):
        cols = slice(128 * c, 128 * (c + 1))
        row = lax.broadcasted_iota(jnp.int32, (capacity, 128), 0)
        terms = jnp.where(row < count_ref[0], coupling_ref[:, cols] * picked[...], 0.0)
        corrected.append(resid_ref[:, cols] - jnp.sum(terms, axis=0, keepdims=True))
    corrected = jnp.concatenate(corrected, axis=1)
    inner = jnp.sum(factor_ref[...] * corrected, axis=1, keepdims=True)
    interior_ref[...] = jnp.sum(factor_ref[...] * inner, axis=0, keepdims=True)


def shards(leaf, blk, interior_factor, coupling, iface_rows, counts, resid_interior, resid_iface, iface_operator):
    factor = interior_factor[0]
    couple = coupling[0]
    capacity, interior = couple.shape
    S = iface_operator.shape[0]
    n = leaf * blk
    vmem = pl.BlockSpec(memory_space=pltpu.VMEM)
    smem = pl.BlockSpec(memory_space=pltpu.SMEM)
    anywhere = pl.BlockSpec(memory_space=pl.ANY)
    size = capacity // 2 + 8

    gathered = pl.pallas_call(
        piece_kernel,
        out_shape=jax.ShapeDtypeStruct((size, 2 * capacity), F32),
        in_specs=[smem, vmem, vmem, vmem, vmem],
        out_specs=vmem,
    )(counts, couple, factor, resid_interior, iface_rows)

    steps = []
    for axis, width, low in (("blk", blk, 0), ("leaf", leaf, blk.bit_length() - 1)):
        for bit in reversed(range(width.bit_length() - 1)):
            other = lax.ppermute(gathered, axis, [(i, i ^ (1 << bit)) for i in range(width)])
            gathered = jnp.concatenate([gathered, other], axis=0)
            steps.append(low + bit)

    me = (lax.axis_index("leaf") * blk + lax.axis_index("blk")).astype(jnp.int32).reshape(1)
    interior_out, iface = pl.pallas_call(
        functools.partial(system_kernel, tuple(steps), n),
        out_shape=(
            jax.ShapeDtypeStruct((1, interior), F32),
            jax.ShapeDtypeStruct((1, S), F32),
        ),
        in_specs=[smem, smem, smem, vmem, anywhere, vmem, vmem, vmem, vmem],
        out_specs=(vmem, vmem),
        scratch_shapes=[
            pltpu.VMEM((S, S), F32),
            pltpu.VMEM((S * 16, 128), F32),
            pltpu.VMEM((capacity * 16, 128), F32),
            pltpu.VMEM((n, 128), F32),
            pltpu.VMEM((n, 128), jnp.int32),
            pltpu.VMEM((n * S // 128, 128), jnp.int32),
            pltpu.VMEM((16, S), F32),
            pltpu.VMEM((S, 3 * NB), BF16),
            pltpu.VMEM((S, 3 * NB), BF16),
            pltpu.VMEM((S, NB), F32),
            pltpu.VMEM((S, 128), F32),
            pltpu.VMEM((capacity, 128), F32),
            pltpu.SMEM((n, 128), jnp.int32),
            pltpu.SemaphoreType.DMA,
            pltpu.SemaphoreType.DMA,
        ],
        compiler_params=pltpu.CompilerParams(vmem_limit_bytes=48 * 1024 * 1024),
    )(
        me,
        iface_rows,
        counts,
        gathered,
        iface_operator,
        resid_iface.reshape(1, S),
        couple,
        factor,
        resid_interior,
    )
    own = S // blk
    own_part = lax.dynamic_slice_in_dim(iface[0], lax.axis_index("blk") * own, own, 0)
    return interior_out, own_part


def solution(mesh):
    spec = ("leaf", "blk")
    return jax.shard_map(
        functools.partial(shards, mesh.shape["leaf"], mesh.shape["blk"]),
        mesh=mesh,
        in_specs=(
            P(spec, None, None),
            P(spec, None, None),
            P(spec, None),
            P(spec),
            P(spec, None),
            P(),
            P(),
        ),
        out_specs=(P(spec, None), P("blk")),
        check_vma=False,
    )
```

```python
import functools
import jax
import jax.numpy as jnp
from jax import lax
from jax.experimental import pallas as pl
from jax.experimental.pallas import tpu as pltpu
from jax.sharding import PartitionSpec as P

F32 = jnp.float32
BF16 = jnp.bfloat16
HIGHEST = lax.Precision.HIGHEST
NB = 128
TB = 256
NT = (((1,), (1,)), ((), ()))


def lane_of(x, j):
    return jnp.broadcast_to(x[:, j : j + 1], (8, 128))


def row_of(x, i):
    return jnp.broadcast_to(x[i : i + 1, :], (8, 128))


def split(x):
    high = x.astype(BF16)
    return high, (x - high.astype(F32)).astype(BF16)


def first_factors(x):
    high, low = split(x)
    return jnp.concatenate([high, high, low], axis=1)


def second_factors(x):
    high, low = split(x)
    return jnp.concatenate([high, low, high], axis=1)


def product(a, b):
    return lax.dot_general(a, b, NT, preferred_element_type=F32)


def inverse_root(T, W):
    T = list(T)
    groups = len(T)
    lane = lax.broadcasted_iota(jnp.int32, (8, 128), 1)
    sub = lax.broadcasted_iota(jnp.int32, (8, 128), 0)
    zero = jnp.zeros((8, 128), F32)
    is_row = [sub == p for p in range(8)]
    own = [lane_of(T[0], j) for j in range(8)]
    after = [lane_of(T[1], j) for j in range(8)]
    ahead = [lane_of(T[1], 8 + j) for j in range(8)]
    for g in range(groups):
        last = g == groups - 1
        inside = (lane >= 8 * g) & (lane < 8 * g + 8)
        t = jnp.where(inside, jnp.where(lane - 8 * g == sub, 1.0, 0.0), T[g])
        w = zero
        inverses = zero
        if not last:
            following = jnp.where(inside, zero, T[g + 1])
        for p in range(8):
            pivot = row_of(own[p], p)
            r = 1.0 / pivot
            f = jnp.where(is_row[p], 0.0, own[p] * r)
            across = [row_of(own[k], p) if k > p else None for k in range(8)]
            u = row_of(t, p)
            if not last:
                scaled = after[p] * r
                for j in range(8):
                    ahead[j] = ahead[j] - scaled * row_of(after[p], j)
                for k in range(p + 1, 8):
                    after[k] = after[k] - scaled * across[k]
                following = following - scaled * u
            for k in range(p + 1, 8):
                own[k] = own[k] - f * across[k]
            w = jnp.where(is_row[p], u * lax.rsqrt(pivot), w)
            t = t - f * u
            inverses = jnp.where(is_row[p], r, inverses)
        W.append(jnp.where(lane < 8 * g + 8, w, 0.0))
        if not last:
            T[g + 1] = following
            own = ahead
        if g + 2 < groups:
            E = t * inverses
            e = [row_of(E, p) for p in range(8)]
            for i in range(g + 2, groups):
                old = T[i]
                terms = [lane_of(old, 8 * g + j) * e[j] for j in range(8)]
                while len(terms) > 1:
                    terms = [x + y for x, y in zip(terms[::2], terms[1::2])]
                T[i] = jnp.where(inside, zero, old) - terms[0]
            after = [lane_of(T[g + 2], 8 * (g + 1) + j) for j in range(8)]
            ahead = [lane_of(T[g + 2], 8 * (g + 2) + j) for j in range(8)]
        yield


def piece_kernel(count_ref, coupling_ref, factor_ref, resid_ref, rows_ref, out_ref):
    capacity, interior = coupling_ref.shape
    active = lax.broadcasted_iota(jnp.int32, (capacity, interior), 0) < count_ref[0]
    coupled = jnp.where(active, coupling_ref[...], 0.0)
    extra = jnp.broadcast_to(resid_ref[...], (8, interior))
    both = jnp.concatenate([coupled, extra], axis=0)
    reduced = lax.dot_general(both, factor_ref[...], NT, precision=HIGHEST, preferred_element_type=F32)
    square = lax.dot_general(reduced, reduced[:capacity], NT, precision=HIGHEST, preferred_element_type=F32)
    half = capacity // 2
    out_ref[0:half, 0:capacity] = square[0:half]
    out_ref[0:half, capacity : 2 * capacity] = square[half:capacity]
    out_ref[half : half + 8, 0:capacity] = square[capacity : capacity + 8]
    out_ref[half : half + 8, capacity : 2 * capacity] = jnp.broadcast_to(
        rows_ref[...].astype(F32), (8, capacity)
    )


def system_kernel(
    steps,
    n,
    me_ref,
    own_rows_ref,
    count_ref,
    pieces_ref,
    operator_ref,
    resid_iface_ref,
    coupling_ref,
    factor_ref,
    resid_ref,
    interior_ref,
    iface_ref,
    M,
    by_row,
    z_rows,
    listed,
    listed_int,
    inverse,
    rhs,
    first,
    second,
    roots,
    x_columns,
    picked,
    listed_smem,
    sem_operator,
    sem_listed,
):
    S = M.shape[0]
    chunks = S // 128
    capacity = coupling_ref.shape[0]
    half = capacity // 2
    size = half + 8
    me = me_ref[0]
    lane = lax.broadcasted_iota(jnp.int32, (8, 128), 1)
    sub = lax.broadcasted_iota(jnp.int32, (8, 128), 0)

    get_operator = pltpu.make_async_copy(operator_ref, M, sem_operator)
    get_operator.start()

    def slot_of(k):
        bits = k ^ me
        slot = 0
        for t, bit in enumerate(steps):
            slot = slot + (((bits >> bit) & 1) << t)
        return slot

    def list_rows(k, carry):
        listed[pl.ds(k, 1), :] = pieces_ref[pl.ds(slot_of(k) * size + half, 1), :]
        return carry

    lax.fori_loop(0, n, list_rows, 0)
    listed_int[...] = listed[...].astype(jnp.int32)
    get_listed = pltpu.make_async_copy(listed_int, listed_smem, sem_listed)
    get_listed.start()

    def clear(i, carry):
        by_row[pl.ds(pl.multiple_of(i * 128, 128), 128), :] = jnp.zeros((128, 128), F32)
        return carry

    lax.fori_loop(0, by_row.shape[0] // 128, clear, 0)

    def invert(b, carry):
        rows8 = listed_int[pl.ds(pl.multiple_of(b * 8, 8), 8), :]
        found = [jnp.full((8, 128), -1, jnp.int32) for _ in range(chunks)]
        for i in range(capacity):
            target = lane_of(rows8, capacity + i)
            for c in range(chunks):
                found[c] = jnp.where(lane + 128 * c == target, i, found[c])
        for c in range(chunks):
            inverse[pl.ds(pl.multiple_of(c * n + b * 8, 8), 8), :] = found[c]
        return carry

    lax.fori_loop(0, n // 8, invert, 0)
    get_listed.wait()

    rhs[...] = jnp.broadcast_to(resid_iface_ref[...], rhs.shape)

    def scatter(k, carry):
        base = slot_of(k) * size
        strips = [pieces_ref[pl.ds(pl.multiple_of(base + 8 * s, 8), 8), :] for s in range(size // 8)]
        for c in range(chunks):
            at = jnp.broadcast_to(inverse[pl.ds(c * n + k, 1), :], (8, 128))
            member = at >= 0
            low = jnp.maximum(at, 0)
            high = low + capacity
            for s in range(half // 8):
                for which, index in ((0, low), (half, high)):
                    spread = jnp.take_along_axis(strips[s], index, axis=1, mode="promise_in_bounds")
                    z_rows[pl.ds((which + 8 * s) * 16 + c, 8, stride=16), :] = jnp.where(member, spread, 0.0)
            spread = jnp.take_along_axis(strips[half // 8], low, axis=1, mode="promise_in_bounds")
            spread = jnp.where(member, spread, 0.0)
            cols = slice(128 * c, 128 * (c + 1))
            rhs[0:8, cols] = rhs[0:8, cols] + spread
        for i in range(0, capacity, 8):
            places = [pl.multiple_of(listed_smem[k, capacity + i + u] * 16, 16) for u in range(8)]
            sums = [
                by_row[pl.ds(places[u], 16), :] + z_rows[16 * (i + u) : 16 * (i + u + 1), :] for u in range(8)
            ]
            for u in range(8):
                by_row[pl.ds(places[u], 16), :] = sums[u]
        return carry

    lax.fori_loop(0, n, scatter, 0)
    rhs[8:16, :] = rhs[0:8, :]
    get_operator.wait()

    def assemble(q, carry):
        row = pl.multiple_of(q * 8, 8)
        for c in range(chunks):
            cols = slice(128 * c, 128 * (c + 1))
            M[pl.ds(row, 8), cols] = M[pl.ds(row, 8), cols] + by_row[pl.ds(row * 16 + c, 8, stride=16), :]
        return carry

    lax.fori_loop(0, S // 8, assemble, 0)

    panels = S // NB

    def block(i):
        return slice(NB * i, NB * (i + 1))

    def finish(p, W):
        W_second = second_factors(W)
        state = {}

        def begin():
            roots[block(p), :] = W.T
            z = product(first_factors(rhs[:, block(p)]), W_second)
            rhs[:, block(p)] = z
            state["z"] = first_factors(z)

        def column(i):
            V = product(first_factors(M[block(i), block(p)]), W_second)
            M[block(i), block(p)] = V
            first[block(i), :] = first_factors(V)
            second[block(i), :] = second_factors(V)

        def right(cols):
            rhs[:, cols] = rhs[:, cols] - product(state["z"], second[cols, :])

        def tile(rows, cols):
            M[rows, cols] = M[rows, cols] - product(first[rows, :], second[cols, :])

        spans = [slice(at, min(at + TB, S)) for at in range(NB * (p + 1), S, TB)]
        work = [begin]
        work += [functools.partial(column, i) for i in range(p + 2, panels)]
        for at, cols in enumerate(spans):
            work.append(functools.partial(right, cols))
            work += [functools.partial(tile, rows, cols) for rows in spans[at:]]
        return work

    work = []
    D = M[block(0), block(0)]
    for j in range(panels):
        W = []
        groups = NB // 8
        done = 0
        for g, _ in enumerate(inverse_root([D[8 * s : 8 * s + 8] for s in range(groups)], W)):
            upto = len(work) * (g + 1) // groups
            for item in work[done:upto]:
                item()
            done = upto
        W = jnp.concatenate(W, axis=0)
        work = finish(j, W)
        if j + 1 < panels:
            V = product(first_factors(M[block(j + 1), block(j)]), second_factors(W))
            M[block(j + 1), block(j)] = V
            V_first, V_second = first_factors(V), second_factors(V)
            first[block(j + 1), :] = V_first
            second[block(j + 1), :] = V_second
            D = M[block(j + 1), block(j + 1)] - product(V_first, V_second)
    for item in work:
        item()

    def back(step, carry):
        j = panels - 1 - step
        at = pl.multiple_of(j * NB, NB)
        t = jnp.broadcast_to(rhs[0:1, pl.ds(at, NB)], (8, NB))
        x = []
        flat = jnp.zeros((8, 128), F32)
        for s in range(NB // 8):
            total = jnp.sum(roots[pl.ds(at + 8 * s, 8), :] * t, axis=1, keepdims=True)
            total = jnp.broadcast_to(total, (8, 128))
            x.append(total)
            x_columns[pl.ds(at + 8 * s, 8), :] = total
            flat = flat + jnp.where(lane == sub + 8 * s, total, 0.0)
        iface_ref[:, pl.ds(at, NB)] = jnp.sum(flat, axis=0, keepdims=True)
        for c in range(chunks):
            cols = slice(128 * c, 128 * (c + 1))
            total = x[0] * M[pl.ds(at, 8), cols]
            for s in range(1, NB // 8):
                total = total + x[s] * M[pl.ds(at + 8 * s, 8), cols]
            rhs[0:1, cols] = rhs[0:1, cols] - jnp.sum(total, axis=0, keepdims=True)
        return carry

    lax.fori_loop(0, panels, back, 0)

    for i in range(capacity):
        picked[i : i + 1, :] = x_columns[pl.ds(own_rows_ref[0, i], 1), :]
    interior = coupling_ref.shape[1]
    corrected = []
    for c in range(interior // 128):
        cols = slice(128 * c, 128 * (c + 1))
        row = lax.broadcasted_iota(jnp.int32, (capacity, 128), 0)
        terms = jnp.where(row < count_ref[0], coupling_ref[:, cols] * picked[...], 0.0)
        corrected.append(resid_ref[:, cols] - jnp.sum(terms, axis=0, keepdims=True))
    corrected = jnp.concatenate(corrected, axis=1)
    inner = jnp.sum(factor_ref[...] * corrected, axis=1, keepdims=True)
    interior_ref[...] = jnp.sum(factor_ref[...] * inner, axis=0, keepdims=True)


def shards(leaf, blk, interior_factor, coupling, iface_rows, counts, resid_interior, resid_iface, iface_operator):
    factor = interior_factor[0]
    couple = coupling[0]
    capacity, interior = couple.shape
    S = iface_operator.shape[0]
    n = leaf * blk
    vmem = pl.BlockSpec(memory_space=pltpu.VMEM)
    smem = pl.BlockSpec(memory_space=pltpu.SMEM)
    anywhere = pl.BlockSpec(memory_space=pl.ANY)
    size = capacity // 2 + 8

    gathered = pl.pallas_call(
        piece_kernel,
        out_shape=jax.ShapeDtypeStruct((size, 2 * capacity), F32),
        in_specs=[smem, vmem, vmem, vmem, vmem],
        out_specs=vmem,
    )(counts, couple, factor, resid_interior, iface_rows)

    steps = []
    for axis, width, low in (("blk", blk, 0), ("leaf", leaf, blk.bit_length() - 1)):
        for bit in reversed(range(width.bit_length() - 1)):
            other = lax.ppermute(gathered, axis, [(i, i ^ (1 << bit)) for i in range(width)])
            gathered = jnp.concatenate([gathered, other], axis=0)
            steps.append(low + bit)

    me = (lax.axis_index("leaf") * blk + lax.axis_index("blk")).astype(jnp.int32).reshape(1)
    interior_out, iface = pl.pallas_call(
        functools.partial(system_kernel, tuple(steps), n),
        out_shape=(
            jax.ShapeDtypeStruct((1, interior), F32),
            jax.ShapeDtypeStruct((1, S), F32),
        ),
        in_specs=[smem, smem, smem, vmem, anywhere, vmem, vmem, vmem, vmem],
        out_specs=(vmem, vmem),
        scratch_shapes=[
            pltpu.VMEM((S, S), F32),
            pltpu.VMEM((S * 16, 128), F32),
            pltpu.VMEM((capacity * 16, 128), F32),
            pltpu.VMEM((n, 128), F32),
            pltpu.VMEM((n, 128), jnp.int32),
            pltpu.VMEM((n * S // 128, 128), jnp.int32),
            pltpu.VMEM((16, S), F32),
            pltpu.VMEM((S, 3 * NB), BF16),
            pltpu.VMEM((S, 3 * NB), BF16),
            pltpu.VMEM((S, NB), F32),
            pltpu.VMEM((S, 128), F32),
            pltpu.VMEM((capacity, 128), F32),
            pltpu.SMEM((n, 128), jnp.int32),
            pltpu.SemaphoreType.DMA,
            pltpu.SemaphoreType.DMA,
        ],
        compiler_params=pltpu.CompilerParams(vmem_limit_bytes=48 * 1024 * 1024),
    )(
        me,
        iface_rows,
        counts,
        gathered,
        iface_operator,
        resid_iface.reshape(1, S),
        couple,
        factor,
        resid_interior,
    )
    own = S // blk
    own_part = lax.dynamic_slice_in_dim(iface[0], lax.axis_index("blk") * own, own, 0)
    return interior_out, own_part


def solution(mesh):
    spec = ("leaf", "blk")
    return jax.shard_map(
        functools.partial(shards, mesh.shape["leaf"], mesh.shape["blk"]),
        mesh=mesh,
        in_specs=(
            P(spec, None, None),
            P(spec, None, None),
            P(spec, None),
            P(spec),
            P(spec, None),
            P(),
            P(),
        ),
        out_specs=(P(spec, None), P("blk")),
        check_vma=False,
    )
```

```python
import functools
import jax
import jax.numpy as jnp
from jax import lax
from jax.experimental import pallas as pl
from jax.experimental.pallas import tpu as pltpu
from jax.sharding import PartitionSpec as P

F32 = jnp.float32
BF16 = jnp.bfloat16
HIGHEST = lax.Precision.HIGHEST
NB = 128
BATCH = 4
TB = 256
NT = (((1,), (1,)), ((), ()))


def lane_of(x, j):
    return jnp.take_along_axis(x, jnp.full((8, 128), j, jnp.int32), axis=1, mode="promise_in_bounds")


def row_of(x, i):
    return jnp.broadcast_to(x[i : i + 1, :], (8, 128))


def split(x):
    high = x.astype(BF16)
    return high, (x - high.astype(F32)).astype(BF16)


def first_factors(x):
    high, low = split(x)
    return jnp.concatenate([high, high, low], axis=1)


def second_factors(x):
    high, low = split(x)
    return jnp.concatenate([high, low, high], axis=1)


def product(a, b):
    return lax.dot_general(a, b, NT, preferred_element_type=F32)


def inverse_root(T, W):
    T = list(T)
    groups = len(T)
    lane = lax.broadcasted_iota(jnp.int32, (8, 128), 1)
    sub = lax.broadcasted_iota(jnp.int32, (8, 128), 0)
    zero = jnp.zeros((8, 128), F32)
    is_row = [sub == p for p in range(8)]
    scaled_rows = []
    own = [lane_of(T[0], j) for j in range(8)]
    after = [lane_of(T[1], j) for j in range(8)]
    ahead = [lane_of(T[1], 8 + j) for j in range(8)]
    for g in range(groups):
        last = g == groups - 1
        inside = (lane >= 8 * g) & (lane < 8 * g + 8)
        t = jnp.where(inside, jnp.where(lane - 8 * g == sub, 1.0, 0.0), T[g])
        w, pivots, inverses = zero, zero, zero
        if not last:
            following = jnp.where(inside, zero, T[g + 1])
        pivot = row_of(own[0], 0)
        for p in range(8):
            r = 1.0 / pivot
            others = jnp.where(is_row[p], 0.0, own[p])
            f = others * r
            across = [row_of(own[k], p) if k > p else None for k in range(8)]
            u = row_of(t, p)
            w = jnp.where(is_row[p], u, w)
            pivots = pivot if p == 0 else jnp.where(is_row[p], pivot, pivots)
            if p < 7:
                own[p + 1] = own[p + 1] - (others * across[p + 1]) * r
                pivot = row_of(own[p + 1], p + 1)
            for k in range(p + 2, 8):
                own[k] = own[k] - f * across[k]
            if not last:
                scaled = after[p] * r
                for j in range(8):
                    ahead[j] = ahead[j] - scaled * row_of(after[p], j)
                for k in range(p + 1, 8):
                    after[k] = after[k] - scaled * across[k]
                following = following - scaled * u
            t = t - f * u
            inverses = jnp.where(is_row[p], r, inverses)
        w = w * lax.rsqrt(pivots)
        scaled_rows.append(w)
        W.append(jnp.where(lane < 8 * g + 8, w, 0.0))
        if not last:
            T[g + 1] = following
            own = ahead
        if g + 2 < groups:
            E = t * inverses
            e = [row_of(E, p) for p in range(8)]
            near = min(groups, BATCH * (g // BATCH + 2))
            for i in range(g + 2, near):
                old = T[i]
                T[i] = jnp.where(inside, zero, old)
                for j in range(8):
                    T[i] = T[i] - lane_of(old, 8 * g + j) * e[j]
            after = [lane_of(T[g + 2], 8 * (g + 1) + j) for j in range(8)]
            ahead = [lane_of(T[g + 2], 8 * (g + 2) + j) for j in range(8)]
            if g % BATCH == BATCH - 1 and near < groups:
                start = g - BATCH + 1
                rows = [
                    jnp.where((lane < 8 * q + 8) | (lane >= 8 * g + 8), scaled_rows[q], 0.0)
                    for q in range(start, g + 1)
                ]
                rows = jnp.concatenate(rows, axis=0)
                high, low = split(rows)
                left_high, left_low = split(rows.T[8 * near : 8 * groups])

                def plain(x, y):
                    return lax.dot_general(x, y, (((1,), (0,)), ((), ())), preferred_element_type=F32)

                far = plain(left_high, high) + (plain(left_high, low) + plain(left_low, high))
                done = (lane >= 8 * start) & (lane < 8 * g + 8)
                for i in range(near, groups):
                    T[i] = jnp.where(done, zero, T[i]) - far[8 * (i - near) : 8 * (i - near) + 8]
        yield


def piece_kernel(count_ref, coupling_ref, factor_ref, resid_ref, piece_ref, rhs_ref):
    capacity, interior = coupling_ref.shape
    active = lax.broadcasted_iota(jnp.int32, (capacity, interior), 0) < count_ref[0]
    coupled = jnp.where(active, coupling_ref[...], 0.0)
    extra = jnp.broadcast_to(resid_ref[...], (8, interior))
    both = jnp.concatenate([coupled, extra], axis=0)
    reduced = lax.dot_general(both, factor_ref[...], NT, precision=HIGHEST, preferred_element_type=F32)
    square = lax.dot_general(reduced, reduced[:capacity], NT, precision=HIGHEST, preferred_element_type=F32)
    half = capacity // 2
    piece_ref[:, 0:capacity] = square[0:half]
    piece_ref[:, capacity : 2 * capacity] = square[half:capacity]
    rhs_ref[...] = square[capacity : capacity + 8]


def system_kernel(
    steps,
    n,
    blk,
    me_ref,
    count_ref,
    pieces_ref,
    operator_hbm,
    resid_iface_hbm,
    coupling_hbm,
    factor_hbm,
    resid_hbm,
    interior_ref,
    iface_ref,
    M,
    by_row,
    z_even,
    z_odd,
    listed,
    listed_int,
    inverse,
    rhs,
    first,
    second,
    roots,
    x_columns,
    picked,
    coupling_ref,
    factor_ref,
    resid_ref,
    resid_iface_ref,
    listed_smem,
    sems,
):
    S = M.shape[0]
    chunks = S // 128
    capacity = coupling_ref.shape[0]
    half = capacity // 2
    size = half + 8
    me = me_ref[0]
    lane = lax.broadcasted_iota(jnp.int32, (8, 128), 1)
    sub = lax.broadcasted_iota(jnp.int32, (8, 128), 0)

    get_operator = pltpu.make_async_copy(operator_hbm, M, sems.at[0])
    get_operator.start()
    get_iface = [
        pltpu.make_async_copy(
            resid_iface_hbm.at[pl.ds(128 * c, 128)], resid_iface_ref.at[c], sems.at[5 + c]
        )
        for c in range(chunks)
    ]
    get_block = [
        pltpu.make_async_copy(coupling_hbm, coupling_ref, sems.at[1]),
        pltpu.make_async_copy(factor_hbm, factor_ref, sems.at[2]),
        pltpu.make_async_copy(resid_hbm, resid_ref, sems.at[3]),
    ]
    for copy in get_iface + get_block:
        copy.start()

    def slot_of(k):
        bits = k ^ me
        slot = 0
        for t, bit in enumerate(steps):
            slot = slot + (((bits >> bit) & 1) << t)
        return slot

    def list_rows(k, carry):
        listed[pl.ds(k, 1), :] = pieces_ref[pl.ds(slot_of(k) * size + half, 1), :]
        return carry

    lax.fori_loop(0, n, list_rows, 0)
    listed_int[...] = listed[...].astype(jnp.int32)
    get_listed = pltpu.make_async_copy(listed_int, listed_smem, sems.at[4])
    get_listed.start()

    def clear(i, carry):
        by_row[pl.ds(pl.multiple_of(i * 128, 128), 128), :] = jnp.zeros((128, 128), F32)
        return carry

    lax.fori_loop(0, by_row.shape[0] // 128, clear, 0)

    def invert(b, carry):
        rows8 = listed_int[pl.ds(pl.multiple_of(b * 8, 8), 8), :]
        found = [jnp.full((8, 128), capacity, jnp.int32) for _ in range(chunks)]
        for i in range(capacity):
            target = lane_of(rows8, capacity + i)
            for c in range(chunks):
                found[c] = jnp.where(lane + 128 * c == target, i, found[c])
        for c in range(chunks):
            inverse[pl.ds(pl.multiple_of(c * n + b * 8, 8), 8), :] = found[c]
        return carry

    lax.fori_loop(0, n // 8, invert, 0)
    get_listed.wait()

    for c, copy in enumerate(get_iface):
        copy.wait()
        rhs[:, 128 * c : 128 * (c + 1)] = jnp.broadcast_to(resid_iface_ref[c : c + 1, :], (16, 128))

    def expand(k, z_rows):
        base = slot_of(k) * size
        strips = [pieces_ref[pl.ds(pl.multiple_of(base + 8 * s, 8), 8), :] for s in range(size // 8)]
        strips = strips[:-1] + [pltpu.roll(x, capacity, 1) for x in strips[:-1]] + strips[-1:]
        lower = lane < capacity
        strips = [jnp.where(lower, x, 0.0) for x in strips]
        for c in range(chunks):
            at = jnp.broadcast_to(inverse[pl.ds(c * n + k, 1), :], (8, 128))
            for s, strip in enumerate(strips):
                spread = jnp.take_along_axis(strip, at, axis=1, mode="promise_in_bounds")
                if s < capacity // 8:
                    z_rows[pl.ds(8 * s * chunks + c, 8, stride=chunks), :] = spread
                else:
                    cols = slice(128 * c, 128 * (c + 1))
                    rhs[0:8, cols] = rhs[0:8, cols] + spread

    def add_rows(k, z_rows):
        for i in range(0, capacity, 8):
            places = [listed_smem[k, capacity + i + u] * chunks for u in range(8)]
            sums = [
                by_row[pl.ds(places[u], chunks), :] + z_rows[chunks * (i + u) : chunks * (i + u + 1), :]
                for u in range(8)
            ]
            for u in range(8):
                by_row[pl.ds(places[u], chunks), :] = sums[u]

    def scatter(pair, carry):
        k = 2 * pair
        expand(k + 1, z_odd)
        add_rows(k, z_even)
        expand(k + 2, z_even)
        add_rows(k + 1, z_odd)
        return carry

    expand(0, z_even)
    lax.fori_loop(0, n // 2 - 1, scatter, 0)
    expand(n - 1, z_odd)
    add_rows(n - 2, z_even)
    add_rows(n - 1, z_odd)
    rhs[8:16, :] = rhs[0:8, :]
    get_operator.wait()

    for part in range(chunks):

        def assemble(q, carry, part=part):
            row = pl.multiple_of(128 * part + q * 8, 8)
            for c in range(part + 1):
                cols = slice(128 * c, 128 * (c + 1))
                M[pl.ds(row, 8), cols] = M[pl.ds(row, 8), cols] + by_row[pl.ds(row * chunks + c, 8, stride=chunks), :]
            return carry

        lax.fori_loop(0, 16, assemble, 0, unroll=2)

    panels = S // NB

    def block(i):
        return slice(NB * i, NB * (i + 1))

    def finish(p, W):
        W_second = second_factors(W)
        state = {}

        def begin():
            roots[block(p), :] = W.T
            z = product(first_factors(rhs[:, block(p)]), W_second)
            rhs[:, block(p)] = z
            state["z"] = first_factors(z)

        def column(i):
            V = product(first_factors(M[block(i), block(p)]), W_second)
            M[block(i), block(p)] = V
            first[block(i), :] = first_factors(V)
            second[block(i), :] = second_factors(V)

        def right(cols):
            rhs[:, cols] = rhs[:, cols] - product(state["z"], second[cols, :])

        def tile(rows, cols):
            M[rows, cols] = M[rows, cols] - product(first[rows, :], second[cols, :])

        spans = [slice(at, min(at + TB, S)) for at in range(NB * (p + 1), S, TB)]
        work = [begin]
        work += [functools.partial(column, i) for i in range(p + 2, panels)]
        for at, cols in enumerate(spans):
            work.append(functools.partial(right, cols))
            work += [functools.partial(tile, rows, cols) for rows in spans[at:]]
        return work

    work = []
    D = M[block(0), block(0)]
    for j in range(panels):
        W = []
        groups = NB // 8
        done = 0
        for g, _ in enumerate(inverse_root([D[8 * s : 8 * s + 8] for s in range(groups)], W)):
            upto = len(work) * (g + 1) // groups
            for item in work[done:upto]:
                item()
            done = upto
        W = jnp.concatenate(W, axis=0)
        work = finish(j, W)
        if j + 1 < panels:
            V = product(first_factors(M[block(j + 1), block(j)]), second_factors(W))
            M[block(j + 1), block(j)] = V
            V_first, V_second = first_factors(V), second_factors(V)
            first[block(j + 1), :] = V_first
            second[block(j + 1), :] = V_second
            D = M[block(j + 1), block(j + 1)] - product(V_first, V_second)
    for item in work:
        item()

    def back(step, carry):
        j = panels - 1 - step
        at = pl.multiple_of(j * NB, NB)
        t = jnp.broadcast_to(rhs[0:1, pl.ds(at, NB)], (8, NB))
        x = []
        for s in range(NB // 8):
            total = jnp.sum(roots[pl.ds(at + 8 * s, 8), :] * t, axis=1, keepdims=True)
            total = jnp.broadcast_to(total, (8, 128))
            x.append(total)
            x_columns[pl.ds(at + 8 * s, 8), :] = total
        for c in range(chunks):
            cols = slice(128 * c, 128 * (c + 1))
            total = x[0] * M[pl.ds(at, 8), cols]
            for s in range(1, NB // 8):
                total = total + x[s] * M[pl.ds(at + 8 * s, 8), cols]
            rhs[0:1, cols] = rhs[0:1, cols] - jnp.sum(total, axis=0, keepdims=True)
        return carry

    lax.fori_loop(0, panels, back, 0)

    own = iface_ref.shape[1]
    begin = (me & (blk - 1)) * own
    for c in range(0, own, 128):
        width = min(128, own - c)
        flat = jnp.zeros((8, 128), F32)
        for s in range(0, width, 8):
            strip = x_columns[pl.ds(pl.multiple_of(begin + c + s, 8), 8), :]
            flat = flat + jnp.where(lane == sub + s, strip, 0.0)
        iface_ref[:, c : c + width] = jnp.sum(flat, axis=0, keepdims=True)[:, :width]

    for copy in get_block:
        copy.wait()
    for i in range(capacity):
        picked[i : i + 1, :] = x_columns[pl.ds(listed_smem[me, capacity + i], 1), :]
    interior = coupling_ref.shape[1]
    corrected = []
    for c in range(interior // 128):
        cols = slice(128 * c, 128 * (c + 1))
        row = lax.broadcasted_iota(jnp.int32, (capacity, 128), 0)
        terms = jnp.where(row < count_ref[0], coupling_ref[:, cols] * picked[...], 0.0)
        corrected.append(resid_ref[:, cols] - jnp.sum(terms, axis=0, keepdims=True))
    corrected = jnp.concatenate(corrected, axis=1)
    inner = jnp.sum(factor_ref[...] * corrected, axis=1, keepdims=True)
    interior_ref[...] = jnp.sum(factor_ref[...] * inner, axis=0, keepdims=True)


def shards(leaf, blk, interior_factor, coupling, iface_rows, counts, resid_interior, resid_iface, iface_operator):
    factor = interior_factor[0]
    couple = coupling[0]
    capacity, interior = couple.shape
    S = iface_operator.shape[0]
    n = leaf * blk
    vmem = pl.BlockSpec(memory_space=pltpu.VMEM)
    smem = pl.BlockSpec(memory_space=pltpu.SMEM)
    anywhere = pl.BlockSpec(memory_space=pl.ANY)
    size = capacity // 2 + 8

    piece, piece_rhs = pl.pallas_call(
        piece_kernel,
        out_shape=(
            jax.ShapeDtypeStruct((capacity // 2, 2 * capacity), F32),
            jax.ShapeDtypeStruct((8, capacity), F32),
        ),
        in_specs=[smem, vmem, vmem, vmem],
        out_specs=(vmem, vmem),
    )(counts, couple, factor, resid_interior)
    listed = jnp.broadcast_to(iface_rows.astype(F32), (8, capacity))
    gathered = jnp.concatenate([piece, jnp.concatenate([piece_rhs, listed], axis=1)], axis=0)

    steps = []
    for axis, width, low in (("blk", blk, 0), ("leaf", leaf, blk.bit_length() - 1)):
        for bit in reversed(range(width.bit_length() - 1)):
            other = lax.ppermute(gathered, axis, [(i, i ^ (1 << bit)) for i in range(width)])
            gathered = jnp.concatenate([gathered, other], axis=0)
            steps.append(low + bit)

    me = (lax.axis_index("leaf") * blk + lax.axis_index("blk")).astype(jnp.int32).reshape(1)
    interior_out, iface = pl.pallas_call(
        functools.partial(system_kernel, tuple(steps), n, blk),
        out_shape=(
            jax.ShapeDtypeStruct((1, interior), F32),
            jax.ShapeDtypeStruct((1, S // blk), F32),
        ),
        in_specs=[smem, smem, vmem] + [anywhere] * 5,
        out_specs=(vmem, vmem),
        scratch_shapes=[
            pltpu.VMEM((S, S), F32),
            pltpu.VMEM((S * S // 128, 128), F32),
            pltpu.VMEM((capacity * S // 128, 128), F32),
            pltpu.VMEM((capacity * S // 128, 128), F32),
            pltpu.VMEM((n, 128), F32),
            pltpu.VMEM((n, 128), jnp.int32),
            pltpu.VMEM((n * S // 128, 128), jnp.int32),
            pltpu.VMEM((16, S), F32),
            pltpu.VMEM((S, 3 * NB), BF16),
            pltpu.VMEM((S, 3 * NB), BF16),
            pltpu.VMEM((S, NB), F32),
            pltpu.VMEM((S, 128), F32),
            pltpu.VMEM((capacity, 128), F32),
            pltpu.VMEM((capacity, interior), F32),
            pltpu.VMEM((interior, interior), F32),
            pltpu.VMEM((1, interior), F32),
            pltpu.VMEM((S // 128, 128), F32),
            pltpu.SMEM((n, 128), jnp.int32),
            pltpu.SemaphoreType.DMA((5 + S // 128,)),
        ],
        compiler_params=pltpu.CompilerParams(vmem_limit_bytes=48 * 1024 * 1024),
    )(
        me,
        counts,
        gathered,
        iface_operator,
        resid_iface,
        couple,
        factor,
        resid_interior,
    )
    return interior_out, iface.reshape(S // blk)


def solution(mesh):
    spec = ("leaf", "blk")
    return jax.shard_map(
        functools.partial(shards, mesh.shape["leaf"], mesh.shape["blk"]),
        mesh=mesh,
        in_specs=(
            P(spec, None, None),
            P(spec, None, None),
            P(spec, None),
            P(spec),
            P(spec, None),
            P(),
            P(),
        ),
        out_specs=(P(spec, None), P("blk")),
        check_vma=False,
    )
```

```python
import functools
import jax
import jax.numpy as jnp
from jax import lax
from jax.experimental import pallas as pl
from jax.experimental.pallas import tpu as pltpu
from jax.sharding import PartitionSpec as P

F32 = jnp.float32
BF16 = jnp.bfloat16
HIGHEST = lax.Precision.HIGHEST
NB = 128
BATCH = 4
TB = 256
NT = (((1,), (1,)), ((), ()))


def lane_of(x, j):
    return jnp.take_along_axis(x, jnp.full((8, 128), j, jnp.int32), axis=1, mode="promise_in_bounds")


def row_of(x, i):
    return jnp.broadcast_to(x[i : i + 1, :], (8, 128))


def split(x):
    high = x.astype(BF16)
    return high, (x - high.astype(F32)).astype(BF16)


def first_factors(x):
    high, low = split(x)
    return jnp.concatenate([high, high, low], axis=1)


def second_factors(x):
    high, low = split(x)
    return jnp.concatenate([high, low, high], axis=1)


def product(a, b):
    return lax.dot_general(a, b, NT, preferred_element_type=F32)


def inverse_root(T, W):
    T = list(T)
    groups = len(T)
    lane = lax.broadcasted_iota(jnp.int32, (8, 128), 1)
    sub = lax.broadcasted_iota(jnp.int32, (8, 128), 0)
    zero = jnp.zeros((8, 128), F32)
    is_row = [sub == p for p in range(8)]
    scaled_rows = []
    own = [lane_of(T[0], j) for j in range(8)]
    after = [lane_of(T[1], j) for j in range(8)]
    ahead = [lane_of(T[1], 8 + j) for j in range(8)]
    for g in range(groups):
        last = g == groups - 1
        inside = (lane >= 8 * g) & (lane < 8 * g + 8)
        t = jnp.where(inside, jnp.where(lane - 8 * g == sub, 1.0, 0.0), T[g])
        w, pivots, inverses = zero, zero, zero
        if not last:
            following = jnp.where(inside, zero, T[g + 1])
        pivot = row_of(own[0], 0)
        for p in range(8):
            r = 1.0 / pivot
            others = jnp.where(is_row[p], 0.0, own[p])
            f = others * r
            across = [row_of(own[k], p) if k > p else None for k in range(8)]
            u = row_of(t, p)
            w = jnp.where(is_row[p], u, w)
            pivots = pivot if p == 0 else jnp.where(is_row[p], pivot, pivots)
            if p < 7:
                own[p + 1] = own[p + 1] - (others * across[p + 1]) * r
                pivot = row_of(own[p + 1], p + 1)
            for k in range(p + 2, 8):
                own[k] = own[k] - f * across[k]
            if not last:
                scaled = after[p] * r
                for j in range(8):
                    ahead[j] = ahead[j] - scaled * row_of(after[p], j)
                for k in range(p + 1, 8):
                    after[k] = after[k] - scaled * across[k]
                following = following - scaled * u
            t = t - f * u
            inverses = jnp.where(is_row[p], r, inverses)
        w = w * lax.rsqrt(pivots)
        scaled_rows.append(w)
        W.append(jnp.where(lane < 8 * g + 8, w, 0.0))
        if not last:
            T[g + 1] = following
            own = ahead
        if g + 2 < groups:
            E = t * inverses
            e = [row_of(E, p) for p in range(8)]
            near = min(groups, BATCH * (g // BATCH + 2))
            for i in range(g + 2, near):
                old = T[i]
                T[i] = jnp.where(inside, zero, old)
                for j in range(8):
                    T[i] = T[i] - lane_of(old, 8 * g + j) * e[j]
            after = [lane_of(T[g + 2], 8 * (g + 1) + j) for j in range(8)]
            ahead = [lane_of(T[g + 2], 8 * (g + 2) + j) for j in range(8)]
            if g % BATCH == BATCH - 1 and near < groups:
                start = g - BATCH + 1
                rows = [
                    jnp.where((lane < 8 * q + 8) | (lane >= 8 * g + 8), scaled_rows[q], 0.0)
                    for q in range(start, g + 1)
                ]
                rows = jnp.concatenate(rows, axis=0)
                high, low = split(rows)
                left_high, left_low = split(rows.T[8 * near : 8 * groups])

                def plain(x, y):
                    return lax.dot_general(x, y, (((1,), (0,)), ((), ())), preferred_element_type=F32)

                far = plain(left_high, high) + (plain(left_high, low) + plain(left_low, high))
                done = (lane >= 8 * start) & (lane < 8 * g + 8)
                for i in range(near, groups):
                    T[i] = jnp.where(done, zero, T[i]) - far[8 * (i - near) : 8 * (i - near) + 8]
        yield


def piece_kernel(
    count_ref,
    coupling_ref,
    factor_ref,
    resid_ref,
    rows_ref,
    resid_iface_hbm,
    out_ref,
    coupled_ref,
    factor_out_ref,
    resid_out_ref,
    iface_out_ref,
    sems,
):
    get_iface = [
        pltpu.make_async_copy(resid_iface_hbm.at[pl.ds(128 * c, 128)], iface_out_ref.at[c], sems.at[c])
        for c in range(iface_out_ref.shape[0])
    ]
    for copy in get_iface:
        copy.start()
    capacity, interior = coupling_ref.shape
    active = lax.broadcasted_iota(jnp.int32, (capacity, interior), 0) < count_ref[0]
    coupled = jnp.where(active, coupling_ref[...], 0.0)
    coupled_ref[...] = coupled
    factor_out_ref[...] = factor_ref[...]
    resid_out_ref[...] = resid_ref[...]
    extra = jnp.broadcast_to(resid_ref[...], (8, interior))
    both = jnp.concatenate([coupled, extra], axis=0)
    reduced = lax.dot_general(both, factor_ref[...], NT, precision=HIGHEST, preferred_element_type=F32)
    square = lax.dot_general(reduced, reduced[:capacity], NT, precision=HIGHEST, preferred_element_type=F32)
    half = capacity // 2
    out_ref[0:half, 0:capacity] = square[0:half]
    out_ref[0:half, capacity : 2 * capacity] = square[half:capacity]
    out_ref[half : half + 8, 0:capacity] = square[capacity : capacity + 8]
    out_ref[half : half + 8, capacity : 2 * capacity] = jnp.broadcast_to(
        rows_ref[...].astype(F32), (8, capacity)
    )
    for copy in get_iface:
        copy.wait()


def system_kernel(
    steps,
    n,
    blk,
    me_ref,
    pieces_ref,
    operator_hbm,
    coupled_ref,
    factor_ref,
    resid_ref,
    resid_iface_ref,
    interior_ref,
    iface_ref,
    M,
    by_row,
    z_even,
    z_odd,
    listed,
    listed_int,
    inverse,
    rhs,
    first,
    second,
    roots,
    x_columns,
    picked,
    listed_smem,
    sems,
):
    S = M.shape[0]
    chunks = S // 128
    capacity = coupled_ref.shape[0]
    half = capacity // 2
    size = half + 8
    me = me_ref[0]
    lane = lax.broadcasted_iota(jnp.int32, (8, 128), 1)
    sub = lax.broadcasted_iota(jnp.int32, (8, 128), 0)

    get_operator = pltpu.make_async_copy(operator_hbm, M, sems.at[0])
    get_operator.start()
    def slot_of(k):
        bits = k ^ me
        slot = 0
        for t, bit in enumerate(steps):
            slot = slot + (((bits >> bit) & 1) << t)
        return slot

    def list_rows(k, carry):
        listed[pl.ds(k, 1), :] = pieces_ref[pl.ds(slot_of(k) * size + half, 1), :]
        return carry

    lax.fori_loop(0, n, list_rows, 0)
    listed_int[...] = listed[...].astype(jnp.int32)
    get_listed = pltpu.make_async_copy(listed_int, listed_smem, sems.at[1])
    get_listed.start()

    def clear(i, carry):
        by_row[pl.ds(pl.multiple_of(i * 128, 128), 128), :] = jnp.zeros((128, 128), F32)
        return carry

    lax.fori_loop(0, by_row.shape[0] // 128, clear, 0)

    def invert(b, carry):
        rows8 = listed_int[pl.ds(pl.multiple_of(b * 8, 8), 8), :]
        found = [jnp.full((8, 128), capacity, jnp.int32) for _ in range(chunks)]
        for i in range(capacity):
            target = lane_of(rows8, capacity + i)
            for c in range(chunks):
                found[c] = jnp.where(lane + 128 * c == target, i, found[c])
        for c in range(chunks):
            inverse[pl.ds(pl.multiple_of(c * n + b * 8, 8), 8), :] = found[c]
        return carry

    lax.fori_loop(0, n // 8, invert, 0)
    get_listed.wait()

    for c in range(chunks):
        rhs[:, 128 * c : 128 * (c + 1)] = jnp.broadcast_to(resid_iface_ref[c : c + 1, :], (16, 128))

    def expand(k, z_rows):
        base = slot_of(k) * size
        strips = [pieces_ref[pl.ds(pl.multiple_of(base + 8 * s, 8), 8), :] for s in range(size // 8)]
        strips = strips[:-1] + [pltpu.roll(x, capacity, 1) for x in strips[:-1]] + strips[-1:]
        lower = lane < capacity
        strips = [jnp.where(lower, x, 0.0) for x in strips]
        for c in range(chunks):
            at = jnp.broadcast_to(inverse[pl.ds(c * n + k, 1), :], (8, 128))
            for s, strip in enumerate(strips):
                spread = jnp.take_along_axis(strip, at, axis=1, mode="promise_in_bounds")
                if s < capacity // 8:
                    z_rows[pl.ds(8 * s * chunks + c, 8, stride=chunks), :] = spread
                else:
                    cols = slice(128 * c, 128 * (c + 1))
                    rhs[0:8, cols] = rhs[0:8, cols] + spread

    def add_rows(k, z_rows):
        for i in range(0, capacity, 8):
            places = [listed_smem[k, capacity + i + u] * chunks for u in range(8)]
            sums = [
                by_row[pl.ds(places[u], chunks), :] + z_rows[chunks * (i + u) : chunks * (i + u + 1), :]
                for u in range(8)
            ]
            for u in range(8):
                by_row[pl.ds(places[u], chunks), :] = sums[u]

    def scatter(pair, carry):
        k = 2 * pair
        expand(k + 1, z_odd)
        add_rows(k, z_even)
        expand(k + 2, z_even)
        add_rows(k + 1, z_odd)
        return carry

    expand(0, z_even)
    lax.fori_loop(0, n // 2 - 1, scatter, 0)
    expand(n - 1, z_odd)
    add_rows(n - 2, z_even)
    add_rows(n - 1, z_odd)
    rhs[8:16, :] = rhs[0:8, :]
    get_operator.wait()

    for part in range(chunks):

        def assemble(q, carry, part=part):
            row = pl.multiple_of(128 * part + q * 8, 8)
            for c in range(part + 1):
                cols = slice(128 * c, 128 * (c + 1))
                M[pl.ds(row, 8), cols] = M[pl.ds(row, 8), cols] + by_row[pl.ds(row * chunks + c, 8, stride=chunks), :]
            return carry

        lax.fori_loop(0, 16, assemble, 0, unroll=2)

    panels = S // NB

    def block(i):
        return slice(NB * i, NB * (i + 1))

    def finish(p, W):
        W_second = second_factors(W)
        state = {}

        def begin():
            roots[block(p), :] = W.T
            z = product(first_factors(rhs[:, block(p)]), W_second)
            rhs[:, block(p)] = z
            state["z"] = first_factors(z)

        def column(i):
            V = product(first_factors(M[block(i), block(p)]), W_second)
            M[block(i), block(p)] = V
            first[block(i), :] = first_factors(V)
            second[block(i), :] = second_factors(V)

        def right(cols):
            rhs[:, cols] = rhs[:, cols] - product(state["z"], second[cols, :])

        def tile(rows, cols):
            M[rows, cols] = M[rows, cols] - product(first[rows, :], second[cols, :])

        spans = [slice(at, min(at + TB, S)) for at in range(NB * (p + 1), S, TB)]
        work = [begin]
        work += [functools.partial(column, i) for i in range(p + 2, panels)]
        for at, cols in enumerate(spans):
            work.append(functools.partial(right, cols))
            work += [functools.partial(tile, rows, cols) for rows in spans[at:]]
        return work

    work = []
    D = M[block(0), block(0)]
    for j in range(panels):
        W = []
        groups = NB // 8
        done = 0
        for g, _ in enumerate(inverse_root([D[8 * s : 8 * s + 8] for s in range(groups)], W)):
            upto = len(work) * (g + 1) // groups
            for item in work[done:upto]:
                item()
            done = upto
        W = jnp.concatenate(W, axis=0)
        work = finish(j, W)
        if j + 1 < panels:
            V = product(first_factors(M[block(j + 1), block(j)]), second_factors(W))
            M[block(j + 1), block(j)] = V
            V_first, V_second = first_factors(V), second_factors(V)
            first[block(j + 1), :] = V_first
            second[block(j + 1), :] = V_second
            D = M[block(j + 1), block(j + 1)] - product(V_first, V_second)
    for item in work:
        item()

    for j in reversed(range(panels)):
        t = jnp.broadcast_to(rhs[0:1, block(j)], (8, NB))
        x = []
        for q in range(NB * j, NB * (j + 1), 8):
            total = jnp.sum(roots[q : q + 8, :] * t, axis=1, keepdims=True)
            x.append(jnp.broadcast_to(total, (8, 128)))
            x_columns[q : q + 8, :] = x[-1]
        for i in reversed(range(j)):
            total = None
            for at, q in enumerate(range(NB * j, NB * (j + 1), 8)):
                term = x[at] * M[q : q + 8, block(i)]
                total = term if total is None else total + term
            rhs[0:1, block(i)] = rhs[0:1, block(i)] - jnp.sum(total, axis=0, keepdims=True)

    own = iface_ref.shape[1]
    begin = (me & (blk - 1)) * own
    for c in range(0, own, 128):
        width = min(128, own - c)
        flat = jnp.zeros((8, 128), F32)
        for s in range(0, width, 8):
            strip = x_columns[pl.ds(pl.multiple_of(begin + c + s, 8), 8), :]
            flat = flat + jnp.where(lane == sub + s, strip, 0.0)
        iface_ref[:, c : c + width] = jnp.sum(flat, axis=0, keepdims=True)[:, :width]

    for i in range(capacity):
        picked[i : i + 1, :] = x_columns[pl.ds(listed_smem[me, capacity + i], 1), :]
    interior = coupled_ref.shape[1]
    corrected = []
    for c in range(interior // 128):
        cols = slice(128 * c, 128 * (c + 1))
        terms = coupled_ref[:, cols] * picked[...]
        corrected.append(resid_ref[:, cols] - jnp.sum(terms, axis=0, keepdims=True))
    corrected = jnp.concatenate(corrected, axis=1)
    inner = jnp.sum(factor_ref[...] * corrected, axis=1, keepdims=True)
    interior_ref[...] = jnp.sum(factor_ref[...] * inner, axis=0, keepdims=True)


def shards(leaf, blk, interior_factor, coupling, iface_rows, counts, resid_interior, resid_iface, iface_operator):
    factor = interior_factor[0]
    couple = coupling[0]
    capacity, interior = couple.shape
    S = iface_operator.shape[0]
    n = leaf * blk
    vmem = pl.BlockSpec(memory_space=pltpu.VMEM)
    smem = pl.BlockSpec(memory_space=pltpu.SMEM)
    anywhere = pl.BlockSpec(memory_space=pltpu.HBM)
    size = capacity // 2 + 8

    gathered, coupled, factor, resid, iface_rhs = pl.pallas_call(
        piece_kernel,
        out_shape=(
            pltpu.VMEM((size, 2 * capacity), F32),
            pltpu.VMEM((capacity, interior), F32),
            pltpu.VMEM((interior, interior), F32),
            pltpu.VMEM((1, interior), F32),
            pltpu.VMEM((S // 128, 128), F32),
        ),
        in_specs=[smem, vmem, vmem, vmem, vmem, anywhere],
        out_specs=(vmem,) * 5,
        scratch_shapes=[pltpu.SemaphoreType.DMA((S // 128,))],
    )(counts, couple, factor, resid_interior, iface_rows, resid_iface)

    steps = []
    for axis, width, low in (("blk", blk, 0), ("leaf", leaf, blk.bit_length() - 1)):
        for bit in reversed(range(width.bit_length() - 1)):
            other = lax.ppermute(gathered, axis, [(i, i ^ (1 << bit)) for i in range(width)])
            gathered = jnp.concatenate([gathered, other], axis=0)
            steps.append(low + bit)

    me = (lax.axis_index("leaf") * blk + lax.axis_index("blk")).astype(jnp.int32).reshape(1)
    interior_out, iface = pl.pallas_call(
        functools.partial(system_kernel, tuple(steps), n, blk),
        out_shape=(
            jax.ShapeDtypeStruct((1, interior), F32),
            jax.ShapeDtypeStruct((1, S // blk), F32),
        ),
        in_specs=[smem, vmem, anywhere, vmem, vmem, vmem, vmem],
        out_specs=(vmem, vmem),
        scratch_shapes=[
            pltpu.VMEM((S, S), F32),
            pltpu.VMEM((S * S // 128, 128), F32),
            pltpu.VMEM((capacity * S // 128, 128), F32),
            pltpu.VMEM((capacity * S // 128, 128), F32),
            pltpu.VMEM((n, 128), F32),
            pltpu.VMEM((n, 128), jnp.int32),
            pltpu.VMEM((n * S // 128, 128), jnp.int32),
            pltpu.VMEM((16, S), F32),
            pltpu.VMEM((S, 3 * NB), BF16),
            pltpu.VMEM((S, 3 * NB), BF16),
            pltpu.VMEM((S, NB), F32),
            pltpu.VMEM((S, 128), F32),
            pltpu.VMEM((capacity, 128), F32),
            pltpu.SMEM((n, 128), jnp.int32),
            pltpu.SemaphoreType.DMA((2,)),
        ],
        compiler_params=pltpu.CompilerParams(vmem_limit_bytes=48 * 1024 * 1024),
    )(
        me,
        gathered,
        iface_operator,
        coupled,
        factor,
        resid,
        iface_rhs,
    )
    return interior_out, iface.reshape(S // blk)


def solution(mesh):
    spec = ("leaf", "blk")
    return jax.shard_map(
        functools.partial(shards, mesh.shape["leaf"], mesh.shape["blk"]),
        mesh=mesh,
        in_specs=(
            P(spec, None, None),
            P(spec, None, None),
            P(spec, None),
            P(spec),
            P(spec, None),
            P(),
            P(),
        ),
        out_specs=(P(spec, None), P("blk")),
        check_vma=False,
    )
```

```python
import functools
import jax
import jax.numpy as jnp
from jax import lax
from jax.experimental import pallas as pl
from jax.experimental.pallas import tpu as pltpu
from jax.sharding import PartitionSpec as P

F32 = jnp.float32
BF16 = jnp.bfloat16
HIGHEST = lax.Precision.HIGHEST
NB = 128
BATCH = 4
TB = 256
NT = (((1,), (1,)), ((), ()))


def lane_of(x, j):
    return jnp.take_along_axis(x, jnp.full((8, 128), j, jnp.int32), axis=1, mode="promise_in_bounds")


def row_of(x, i):
    return jnp.broadcast_to(x[i : i + 1, :], (8, 128))


def split(x):
    high = x.astype(BF16)
    return high, (x - high.astype(F32)).astype(BF16)


def first_factors(x):
    high, low = split(x)
    return jnp.concatenate([high, high, low], axis=1)


def second_factors(x):
    high, low = split(x)
    return jnp.concatenate([high, low, high], axis=1)


def product(a, b):
    return lax.dot_general(a, b, NT, preferred_element_type=F32)


def inverse_root(T, W):
    T = list(T)
    groups = len(T)
    lane = lax.broadcasted_iota(jnp.int32, (8, 128), 1)
    sub = lax.broadcasted_iota(jnp.int32, (8, 128), 0)
    zero = jnp.zeros((8, 128), F32)
    is_row = [sub == p for p in range(8)]
    scaled_rows = []
    own = [lane_of(T[0], j) for j in range(8)]
    after = [lane_of(T[1], j) for j in range(8)]
    ahead = [lane_of(T[1], 8 + j) for j in range(8)]
    for g in range(groups):
        last = g == groups - 1
        inside = (lane >= 8 * g) & (lane < 8 * g + 8)
        t = jnp.where(inside, jnp.where(lane - 8 * g == sub, 1.0, 0.0), T[g])
        w, pivots, inverses = zero, zero, zero
        if not last:
            following = jnp.where(inside, zero, T[g + 1])
        pivot = row_of(own[0], 0)
        for p in range(8):
            r = 1.0 / pivot
            others = jnp.where(is_row[p], 0.0, own[p])
            f = others * r
            across = [row_of(own[k], p) if k > p else None for k in range(8)]
            u = row_of(t, p)
            w = jnp.where(is_row[p], u, w)
            pivots = pivot if p == 0 else jnp.where(is_row[p], pivot, pivots)
            if p < 7:
                own[p + 1] = own[p + 1] - (others * across[p + 1]) * r
                pivot = row_of(own[p + 1], p + 1)
            for k in range(p + 2, 8):
                own[k] = own[k] - f * across[k]
            if not last:
                scaled = after[p] * r
                for j in range(8):
                    ahead[j] = ahead[j] - scaled * row_of(after[p], j)
                for k in range(p + 1, 8):
                    after[k] = after[k] - scaled * across[k]
                following = following - scaled * u
            t = t - f * u
            inverses = jnp.where(is_row[p], r, inverses)
        w = w * lax.rsqrt(pivots)
        scaled_rows.append(w)
        W.append(jnp.where(lane < 8 * g + 8, w, 0.0))
        if not last:
            T[g + 1] = following
            own = ahead
        if g + 2 < groups:
            E = t * inverses
            e = [row_of(E, p) for p in range(8)]
            near = min(groups, BATCH * (g // BATCH + 2))
            for i in range(g + 2, near):
                old = T[i]
                T[i] = jnp.where(inside, zero, old)
                for j in range(8):
                    T[i] = T[i] - lane_of(old, 8 * g + j) * e[j]
            after = [lane_of(T[g + 2], 8 * (g + 1) + j) for j in range(8)]
            ahead = [lane_of(T[g + 2], 8 * (g + 2) + j) for j in range(8)]
            if g % BATCH == BATCH - 1 and near < groups:
                start = g - BATCH + 1
                rows = [
                    jnp.where((lane < 8 * q + 8) | (lane >= 8 * g + 8), scaled_rows[q], 0.0)
                    for q in range(start, g + 1)
                ]
                rows = jnp.concatenate(rows, axis=0)
                high, low = split(rows)
                left_high, left_low = high[:, 8 * near : 8 * groups], low[:, 8 * near : 8 * groups]

                def plain(x, y):
                    return lax.dot_general(x, y, (((0,), (0,)), ((), ())), preferred_element_type=F32)

                far = plain(left_high, high) + (plain(left_high, low) + plain(left_low, high))
                done = (lane >= 8 * start) & (lane < 8 * g + 8)
                for i in range(near, groups):
                    T[i] = jnp.where(done, zero, T[i]) - far[8 * (i - near) : 8 * (i - near) + 8]
        yield


def piece_kernel(
    count_ref,
    coupling_ref,
    factor_ref,
    resid_ref,
    rows_ref,
    resid_iface_hbm,
    out_ref,
    coupled_ref,
    factor_out_ref,
    resid_out_ref,
    iface_out_ref,
    sems,
):
    get_iface = [
        pltpu.make_async_copy(resid_iface_hbm.at[pl.ds(128 * c, 128)], iface_out_ref.at[c], sems.at[c])
        for c in range(iface_out_ref.shape[0])
    ]
    for copy in get_iface:
        copy.start()
    capacity, interior = coupling_ref.shape
    active = lax.broadcasted_iota(jnp.int32, (capacity, interior), 0) < count_ref[0]
    coupled = jnp.where(active, coupling_ref[...], 0.0)
    coupled_ref[...] = coupled
    factor_out_ref[...] = factor_ref[...]
    resid_out_ref[...] = resid_ref[...]
    extra = jnp.broadcast_to(resid_ref[...], (8, interior))
    both = jnp.concatenate([coupled, extra], axis=0)
    reduced = lax.dot_general(both, factor_ref[...], NT, precision=HIGHEST, preferred_element_type=F32)
    square = lax.dot_general(reduced, reduced[:capacity], NT, precision=HIGHEST, preferred_element_type=F32)
    half = capacity // 2
    out_ref[0:half, 0:capacity] = square[0:half]
    out_ref[0:half, capacity : 2 * capacity] = square[half:capacity]
    out_ref[half : half + 8, 0:capacity] = square[capacity : capacity + 8]
    out_ref[half : half + 8, capacity : 2 * capacity] = jnp.broadcast_to(
        rows_ref[...].astype(F32), (8, capacity)
    )
    for copy in get_iface:
        copy.wait()


def system_kernel(
    steps,
    n,
    blk,
    me_ref,
    pieces_ref,
    operator_hbm,
    coupled_ref,
    factor_ref,
    resid_ref,
    resid_iface_ref,
    interior_ref,
    iface_ref,
    M,
    by_row,
    z_even,
    z_odd,
    listed,
    listed_int,
    inverse,
    rhs,
    first,
    second,
    roots,
    x_columns,
    picked,
    listed_smem,
    sems,
):
    S = M.shape[0]
    chunks = S // 128
    capacity = coupled_ref.shape[0]
    half = capacity // 2
    size = half + 8
    me = me_ref[0]
    lane = lax.broadcasted_iota(jnp.int32, (8, 128), 1)
    sub = lax.broadcasted_iota(jnp.int32, (8, 128), 0)

    get_operator = pltpu.make_async_copy(operator_hbm, M, sems.at[0])
    get_operator.start()
    def slot_of(k):
        bits = k ^ me
        slot = 0
        for t, bit in enumerate(steps):
            slot = slot + (((bits >> bit) & 1) << t)
        return slot

    def list_rows(k, carry):
        listed[pl.ds(k, 1), :] = pieces_ref[pl.ds(slot_of(k) * size + half, 1), :]
        return carry

    lax.fori_loop(0, n, list_rows, 0)
    listed_int[...] = listed[...].astype(jnp.int32)
    get_listed = pltpu.make_async_copy(listed_int, listed_smem, sems.at[1])
    get_listed.start()

    def clear(i, carry):
        by_row[pl.ds(pl.multiple_of(i * 128, 128), 128), :] = jnp.zeros((128, 128), F32)
        return carry

    lax.fori_loop(0, by_row.shape[0] // 128, clear, 0)

    def invert(b, carry):
        rows8 = listed_int[pl.ds(pl.multiple_of(b * 8, 8), 8), :]
        found = [jnp.full((8, 128), capacity, jnp.int32) for _ in range(chunks)]
        for i in range(capacity):
            target = lane_of(rows8, capacity + i)
            for c in range(chunks):
                found[c] = jnp.where(lane + 128 * c == target, i, found[c])
        for c in range(chunks):
            inverse[pl.ds(pl.multiple_of(c * n + b * 8, 8), 8), :] = found[c]
        return carry

    lax.fori_loop(0, n // 8, invert, 0)
    get_listed.wait()

    for c in range(chunks):
        rhs[:, 128 * c : 128 * (c + 1)] = jnp.broadcast_to(resid_iface_ref[c : c + 1, :], (16, 128))

    def expand(k, z_rows):
        base = slot_of(k) * size
        strips = [pieces_ref[pl.ds(pl.multiple_of(base + 8 * s, 8), 8), :] for s in range(size // 8)]
        strips = strips[:-1] + [pltpu.roll(x, capacity, 1) for x in strips[:-1]] + strips[-1:]
        lower = lane < capacity
        strips = [jnp.where(lower, x, 0.0) for x in strips]
        for c in range(chunks):
            at = jnp.broadcast_to(inverse[pl.ds(c * n + k, 1), :], (8, 128))
            for s, strip in enumerate(strips):
                spread = jnp.take_along_axis(strip, at, axis=1, mode="promise_in_bounds")
                if s < capacity // 8:
                    z_rows[pl.ds(8 * s * chunks + c, 8, stride=chunks), :] = spread
                else:
                    cols = slice(128 * c, 128 * (c + 1))
                    rhs[0:8, cols] = rhs[0:8, cols] + spread

    def add_rows(k, z_rows):
        for i in range(0, capacity, 8):
            places = [listed_smem[k, capacity + i + u] * chunks for u in range(8)]
            sums = [
                by_row[pl.ds(places[u], chunks), :] + z_rows[chunks * (i + u) : chunks * (i + u + 1), :]
                for u in range(8)
            ]
            for u in range(8):
                by_row[pl.ds(places[u], chunks), :] = sums[u]

    def scatter(pair, carry):
        k = 2 * pair
        expand(k + 1, z_odd)
        add_rows(k, z_even)
        expand(k + 2, z_even)
        add_rows(k + 1, z_odd)
        return carry

    expand(0, z_even)
    lax.fori_loop(0, n // 2 - 1, scatter, 0)
    expand(n - 1, z_odd)
    add_rows(n - 2, z_even)
    add_rows(n - 1, z_odd)
    rhs[8:16, :] = rhs[0:8, :]
    get_operator.wait()

    for part in range(chunks):

        def assemble(q, carry, part=part):
            row = pl.multiple_of(128 * part + q * 8, 8)
            for c in range(part + 1):
                cols = slice(128 * c, 128 * (c + 1))
                M[pl.ds(row, 8), cols] = M[pl.ds(row, 8), cols] + by_row[pl.ds(row * chunks + c, 8, stride=chunks), :]
            return carry

        lax.fori_loop(0, 16, assemble, 0, unroll=2)

    panels = S // NB

    def block(i):
        return slice(NB * i, NB * (i + 1))

    def finish(p, W):
        W_second = second_factors(W)
        state = {}

        def begin():
            roots[block(p), :] = W.T
            z = product(first_factors(rhs[:, block(p)]), W_second)
            rhs[:, block(p)] = z
            state["z"] = first_factors(z)

        def column(i):
            V = product(first_factors(M[block(i), block(p)]), W_second)
            M[block(i), block(p)] = V
            first[block(i), :] = first_factors(V)
            second[block(i), :] = second_factors(V)

        def right(cols):
            rhs[:, cols] = rhs[:, cols] - product(state["z"], second[cols, :])

        def tile(rows, cols):
            M[rows, cols] = M[rows, cols] - product(first[rows, :], second[cols, :])

        spans = [slice(at, min(at + TB, S)) for at in range(NB * (p + 1), S, TB)]
        work = [begin]
        work += [functools.partial(column, i) for i in range(p + 2, panels)]
        for cols in spans:
            work.append(functools.partial(right, cols))
            work.append(functools.partial(tile, slice(cols.start, S), cols))
        return work

    work = []
    D = M[block(0), block(0)]
    for j in range(panels):
        W = []
        groups = NB // 8
        done = 0
        for g, _ in enumerate(inverse_root([D[8 * s : 8 * s + 8] for s in range(groups)], W)):
            upto = len(work) * (g + 1) // groups
            for item in work[done:upto]:
                item()
            done = upto
        W = jnp.concatenate(W, axis=0)
        work = finish(j, W)
        if j + 1 < panels:
            V = product(first_factors(M[block(j + 1), block(j)]), second_factors(W))
            M[block(j + 1), block(j)] = V
            V_first, V_second = first_factors(V), second_factors(V)
            first[block(j + 1), :] = V_first
            second[block(j + 1), :] = V_second
            D = M[block(j + 1), block(j + 1)] - product(V_first, V_second)
    for item in work:
        item()

    for j in reversed(range(panels)):
        t = jnp.broadcast_to(rhs[0:1, block(j)], (8, NB))
        x = []
        for q in range(NB * j, NB * (j + 1), 8):
            total = jnp.sum(roots[q : q + 8, :] * t, axis=1, keepdims=True)
            x.append(jnp.broadcast_to(total, (8, 128)))
            x_columns[q : q + 8, :] = x[-1]
        for i in reversed(range(j)):
            total = None
            for at, q in enumerate(range(NB * j, NB * (j + 1), 8)):
                term = x[at] * M[q : q + 8, block(i)]
                total = term if total is None else total + term
            rhs[0:1, block(i)] = rhs[0:1, block(i)] - jnp.sum(total, axis=0, keepdims=True)

    own = iface_ref.shape[1]
    begin = (me & (blk - 1)) * own
    for c in range(0, own, 128):
        width = min(128, own - c)
        flat = jnp.zeros((8, 128), F32)
        for s in range(0, width, 8):
            strip = x_columns[pl.ds(pl.multiple_of(begin + c + s, 8), 8), :]
            flat = flat + jnp.where(lane == sub + s, strip, 0.0)
        iface_ref[:, c : c + width] = jnp.sum(flat, axis=0, keepdims=True)[:, :width]

    for i in range(capacity):
        picked[i : i + 1, :] = x_columns[pl.ds(listed_smem[me, capacity + i], 1), :]
    interior = coupled_ref.shape[1]
    corrected = []
    for c in range(interior // 128):
        cols = slice(128 * c, 128 * (c + 1))
        terms = coupled_ref[:, cols] * picked[...]
        corrected.append(resid_ref[:, cols] - jnp.sum(terms, axis=0, keepdims=True))
    corrected = jnp.concatenate(corrected, axis=1)
    inner = jnp.sum(factor_ref[...] * corrected, axis=1, keepdims=True)
    interior_ref[...] = jnp.sum(factor_ref[...] * inner, axis=0, keepdims=True)


def shards(leaf, blk, interior_factor, coupling, iface_rows, counts, resid_interior, resid_iface, iface_operator):
    factor = interior_factor[0]
    couple = coupling[0]
    capacity, interior = couple.shape
    S = iface_operator.shape[0]
    n = leaf * blk
    vmem = pl.BlockSpec(memory_space=pltpu.VMEM)
    smem = pl.BlockSpec(memory_space=pltpu.SMEM)
    anywhere = pl.BlockSpec(memory_space=pltpu.HBM)
    size = capacity // 2 + 8

    gathered, coupled, factor, resid, iface_rhs = pl.pallas_call(
        piece_kernel,
        out_shape=(
            pltpu.VMEM((size, 2 * capacity), F32),
            pltpu.VMEM((capacity, interior), F32),
            pltpu.VMEM((interior, interior), F32),
            pltpu.VMEM((1, interior), F32),
            pltpu.VMEM((S // 128, 128), F32),
        ),
        in_specs=[smem, vmem, vmem, vmem, vmem, anywhere],
        out_specs=(vmem,) * 5,
        scratch_shapes=[pltpu.SemaphoreType.DMA((S // 128,))],
    )(counts, couple, factor, resid_interior, iface_rows, resid_iface)

    steps = []
    for axis, width, low in (("blk", blk, 0), ("leaf", leaf, blk.bit_length() - 1)):
        for bit in reversed(range(width.bit_length() - 1)):
            other = lax.ppermute(gathered, axis, [(i, i ^ (1 << bit)) for i in range(width)])
            gathered = jnp.concatenate([gathered, other], axis=0)
            steps.append(low + bit)

    me = (lax.axis_index("leaf") * blk + lax.axis_index("blk")).astype(jnp.int32).reshape(1)
    interior_out, iface = pl.pallas_call(
        functools.partial(system_kernel, tuple(steps), n, blk),
        out_shape=(
            jax.ShapeDtypeStruct((1, interior), F32),
            jax.ShapeDtypeStruct((1, S // blk), F32),
        ),
        in_specs=[smem, vmem, anywhere, vmem, vmem, vmem, vmem],
        out_specs=(vmem, vmem),
        scratch_shapes=[
            pltpu.VMEM((S, S), F32),
            pltpu.VMEM((S * S // 128, 128), F32),
            pltpu.VMEM((capacity * S // 128, 128), F32),
            pltpu.VMEM((capacity * S // 128, 128), F32),
            pltpu.VMEM((n, 128), F32),
            pltpu.VMEM((n, 128), jnp.int32),
            pltpu.VMEM((n * S // 128, 128), jnp.int32),
            pltpu.VMEM((16, S), F32),
            pltpu.VMEM((S, 3 * NB), BF16),
            pltpu.VMEM((S, 3 * NB), BF16),
            pltpu.VMEM((S, NB), F32),
            pltpu.VMEM((S, 128), F32),
            pltpu.VMEM((capacity, 128), F32),
            pltpu.SMEM((n, 128), jnp.int32),
            pltpu.SemaphoreType.DMA((2,)),
        ],
        compiler_params=pltpu.CompilerParams(vmem_limit_bytes=48 * 1024 * 1024),
    )(
        me,
        gathered,
        iface_operator,
        coupled,
        factor,
        resid,
        iface_rhs,
    )
    return interior_out, iface.reshape(S // blk)


def solution(mesh):
    spec = ("leaf", "blk")
    return jax.shard_map(
        functools.partial(shards, mesh.shape["leaf"], mesh.shape["blk"]),
        mesh=mesh,
        in_specs=(
            P(spec, None, None),
            P(spec, None, None),
            P(spec, None),
            P(spec),
            P(spec, None),
            P(),
            P(),
        ),
        out_specs=(P(spec, None), P("blk")),
        check_vma=False,
    )
```
